128 devices in a mesh: dp: 8 (over z, core), space: 16 (over x, y).
Axes of the slice: x: 4, y: 4, z: 4, core: 2. Of those that a mesh axis runs over, the one named last changes fastest.
Arguments:
- feats: bfloat16 [16, 128, 128, 1536], P('dp', 'space'), may hold values from -6 to 6
- lateral: bfloat16 [1536, 512], replicated, may hold values from -0.15625 to 0.15625
- kernel: float32 [7, 7, 512], replicated, may hold values from -0.875 to 0.875
- grad_out: bfloat16 [16, 128, 128, 512], P('dp', 'space'), may hold values from -6 to 6
- error: float32 [196608, 512], P(('dp', 'space')), may hold values from -192 to 192
- q_prev: float32 [512, 8], replicated, may hold values from -6 to 6
Outputs:
- smoothed: bfloat16 [16, 128, 128, 512], P('dp', 'space')
- grad_feats: bfloat16 [16, 128, 128, 1536], P('dp', 'space')
- q_next: float32 [512, 8], replicated
- update: float32 [1536, 512], P('space')
- error_next: float32 [196608, 512], P(('dp', 'space'))
The draws below stay inside these ranges and needn't reach their ends.
All inputs are finite; a program needn't handle non-finite values.
Results may differ from the reference program's by a relative error of at most 0.0049.
Values may be sent and summed in bfloat16 or wider, within the bound.
A program may use at most 128 MiB of HBM per device.

```python
import jax
import jax.numpy as jnp
from jax import lax

C = 1536
F = 512
RANK = 8
KS = 7
TILES_DEV = 2
ROWS_DEV = 8
WID = 128
BATCH = 16
H = 128
WORKERS = 128
N_DP = 8
N_SPACE = 16


def steps_of(key, dims, cuts, least, high):
    factor_of = 1.0
    for axis_at, shards_of in cuts:
        heights = jax.random.uniform(jax.random.fold_in(jax.random.fold_in(key, 6), axis_at), (shards_of,), jnp.float32, least / len(cuts), high / len(cuts))
        factor_of = factor_of * jnp.repeat(jnp.exp(heights), dims[axis_at] // shards_of).reshape((-1,) + (1,) * (len(dims) - 1 - axis_at))
    return factor_of


def noise(rng, dims, width, most, shards=(), dtype=jnp.bfloat16):
    gain = steps_of(rng, dims, shards, -0.22, 0.18) if shards else 1.0
    entries = jax.random.normal(rng, dims, jnp.float32) * width * gain
    return jnp.minimum(jnp.maximum(entries, -most), most).astype(dtype)


def setup_inputs(seed: int = 0) -> dict:
    streams_of = jax.random.split(jax.random.key(seed), 7)
    feats = noise(streams_of[0], (BATCH, H, WID, C), 1.0, 6.0, ((0, 8), (1, 16)))
    lateral = noise(streams_of[1], (C, F), C ** -0.5, 0.15625)
    kernel = noise(streams_of[2], (KS, KS, F), (KS * KS) ** -0.5, 0.875, (), jnp.float32)
    grad_out = noise(streams_of[3], (BATCH, H, WID, F), 1.0, 6.0, ((0, 8), (1, 16)))
    error = noise(streams_of[4], (WORKERS * C, F), 32.0, 192.0, ((0, 128),), jnp.float32)
    q_prev = noise(streams_of[5], (F, RANK), 1.0, 6.0, (), jnp.float32)
    return dict(feats=feats, lateral=lateral, kernel=kernel, grad_out=grad_out, error=error, q_prev=q_prev)


def depthwise(padded, kernel, rows, cols, flip):
    size = kernel.shape[0]
    total = jnp.zeros(padded.shape[:1] + (rows, cols, padded.shape[3]), jnp.float32)
    for a in range(size):
        for c in range(size):
            if flip:
                top, left = (size - 1 - a, size - 1 - c)
            else:
                top, left = (a, c)
            piece = padded[:, top:top + rows, left:left + cols, :].astype(jnp.float32)
            total = total + kernel[a, c] * piece
    return total

def orthonormal(matrix):
    finished = []
    for index in range(matrix.shape[1]):
        column = matrix[:, index]
        for other in finished:
            column = column - jnp.sum(other * column) * other
        column = column / jnp.sqrt(jnp.sum(column * column) + 1e-06)
        finished.append(column)
    return jnp.stack(finished, axis=1)

def reference(feats, lateral, kernel, grad_out, error, q_prev):
    half = KS // 2
    highest = lax.Precision.HIGHEST
    flat = feats.reshape(-1, C)
    projected = jnp.dot(flat, lateral, preferred_element_type=jnp.float32).astype(jnp.bfloat16)
    projected = projected.reshape(BATCH, H, WID, F)
    pad_width = ((0, 0), (half, half), (half, half), (0, 0))
    smoothed = depthwise(jnp.pad(projected, pad_width), kernel, H, WID, False).astype(jnp.bfloat16)
    grad_proj = depthwise(jnp.pad(grad_out, pad_width), kernel, H, WID, True).astype(jnp.bfloat16)
    grad_feats = jnp.dot(grad_proj.reshape(-1, F), lateral.T, preferred_element_type=jnp.float32)
    grad_feats = grad_feats.astype(jnp.bfloat16).reshape(BATCH, H, WID, C)
    cells = TILES_DEV * ROWS_DEV * WID
    worker_feats = feats.reshape(N_DP, TILES_DEV, N_SPACE, ROWS_DEV, WID, C).transpose(0, 2, 1, 3, 4, 5).reshape(N_DP * N_SPACE, cells, C)
    worker_grads = grad_proj.reshape(N_DP, TILES_DEV, N_SPACE, ROWS_DEV, WID, F).transpose(0, 2, 1, 3, 4, 5).reshape(N_DP * N_SPACE, cells, F)

    def one_worker(pair):
        return lax.dot_general(pair[0], pair[1], (((0,), (0,)), ((), ())), preferred_element_type=jnp.float32)
    gradients = lax.map(one_worker, (worker_feats, worker_grads))
    matrices = gradients + error.reshape(N_DP * N_SPACE, C, F)
    count = N_DP * N_SPACE
    left = jnp.einsum('wcf,fr->cr', matrices, q_prev, precision=highest) / count
    basis = orthonormal(left)
    q_next = jnp.einsum('wcf,cr->fr', matrices, basis, precision=highest) / count
    update = jnp.dot(basis, q_next.T, precision=highest)
    error_next = (matrices - update[None]).reshape(count * C, F)
    return (smoothed, grad_feats, q_next, update, error_next)
```

```python
import jax
import jax.numpy as jnp
from jax import lax
from jax.experimental import pallas as pl
from jax.experimental.pallas import tpu as pltpu
from jax.sharding import PartitionSpec as P

MESH = pl.DeviceIdType.MESH
BF = jnp.bfloat16
F32 = jnp.float32
TAPS = 7
HALF = 3
LEAVES = 26
SEG = 16
SEGS = 8
EXT = (SEG + 2 * HALF) * SEGS
PIECES = 8
WINDOW = 3


def leaf_inputs(d):
    if len(d) == 1:
        return [d[0]]
    size = (len(d) + 1) // 2
    half, span = size // 2, size - 1
    sub = lambda x, y: None if x is None or y is None else x - y
    d0, d1, d2 = d[:span], d[half : half + span], d[size : size + span]
    first = [sub(x, y) for x, y in zip(d0, d1)]
    last = [sub(x, y) for x, y in zip(d2, d1)]
    return leaf_inputs(first) + leaf_inputs(d1) + leaf_inputs(last)


def leaf_weights(h):
    if len(h) == 1:
        return [h[0]]
    half = len(h) // 2
    low, high = h[:half], h[half:]
    both = [x if y is None else x + y for x, y in zip(low, high)]
    return leaf_weights(low) + leaf_weights(both) + leaf_weights(high)


def leaf_outputs(m):
    if len(m) == 1:
        return [m[0]]
    third = len(m) // 3
    first, mid, last = (leaf_outputs(m[i * third : (i + 1) * third]) for i in range(3))
    add = lambda x, y: x if y is None else x + y
    return [add(y, x) for x, y in zip(first, mid)] + [add(x, y) for x, y in zip(mid, last)]


def split(x):
    high = x.astype(BF)
    return high, (x - high.astype(F32)).astype(BF)


def stacked(x):
    high = x.astype(BF).astype(F32)
    return jnp.concatenate([high, x - high], axis=0).astype(BF)


def nt(x, y):
    return lax.dot_general(x, y, (((1,), (1,)), ((), ())), preferred_element_type=F32)


def fold(x):
    return x[:8] + x[8:16]


def main_kernel(
    feats_h, lateral_h, grad_h, error_h, kernel_ref, q_ref,
    gp_h, sm_h, basis_ref, qt_ref,
    feats, lateral, grad, error, proj, gp, sm,
    halo_g, halo_p, own_g, own_p, rims, leaf_u, leaf_v, weights, pieces,
    p_buf, p_rs, p_part, p_all, p_out, r_buf, r_rs, r_part, r_all, r_out,
    in_sem, feats_sem, out_sem, halo_send, halo_recv, send1, recv1, send2, recv2, send3, recv3,
):
    s, d = lax.axis_index("space"), lax.axis_index("dp")
    n_s, n_d = 16, 8
    up, down = lax.rem(s + 1, n_s), lax.rem(s + n_s - 1, n_s)
    chunk_rows = 256

    cp_grad = pltpu.make_async_copy(grad_h, grad, in_sem.at[0])
    cp_lat = pltpu.make_async_copy(lateral_h, lateral, in_sem.at[1])
    cp_err = pltpu.make_async_copy(error_h, error, in_sem.at[2])
    cp_grad.start()
    cp_lat.start()

    def feats_copy(i):
        rows = pl.ds(pl.multiple_of(i * chunk_rows, chunk_rows), chunk_rows)
        return pltpu.make_async_copy(feats_h.at[rows], feats.at[rows], feats_sem.at[i])

    @pl.loop(0, 8)
    def _(i):
        feats_copy(i).start()

    cp_err.start()

    barrier = pltpu.get_barrier_semaphore()

    @pl.loop(1, n_s)
    def _(i):
        pl.semaphore_signal(barrier, inc=1, device_id={"space": lax.rem(s + i, n_s)}, device_id_type=MESH)

    @pl.loop(1, n_d)
    def _(i):
        pl.semaphore_signal(barrier, inc=1, device_id={"dp": lax.rem(d + i, n_d)}, device_id_type=MESH)

    pl.semaphore_wait(barrier, n_s - 1 + n_d - 1)

    def rim_copy(which, k, side):
        tile = lax.rem(k, 2)
        lanes = pl.ds(pl.multiple_of((k // 2) * 128, 128), 128)
        source, target = (grad_h, halo_g) if which == 0 else (proj, halo_p)
        rows = pl.ds(5, 3) if side == 0 else pl.ds(0, 3)
        at = (which * PIECES + k) * 2 + side
        return pltpu.make_async_remote_copy(
            src_ref=source.at[tile, rows, :, lanes],
            dst_ref=target.at[side, tile, :, :, lanes],
            send_sem=halo_send.at[at],
            recv_sem=halo_recv.at[at],
            device_id={"space": up if side == 0 else down},
            device_id_type=MESH,
        )

    def rim_start(which, k):
        rim_copy(which, k, 0).start()
        rim_copy(which, k, 1).start()

    def rim_wait(which, k):
        rim_copy(which, k, 0).wait()
        rim_copy(which, k, 1).wait()

    for k in range(WINDOW):
        rim_start(0, k)

    row = lax.broadcasted_iota(jnp.int32, (EXT, 128), 0)
    col = lax.broadcasted_iota(jnp.int32, (EXT, 128), 1)
    spread = jnp.where((row % 8) * SEG + row // 8 - HALF == col, 1.0, 0.0).astype(BF)
    row = lax.broadcasted_iota(jnp.int32, (128, 128), 0)
    col = lax.broadcasted_iota(jnp.int32, (128, 128), 1)
    gather = jnp.where((col % 8) * SEG + col // 8 == row, 1.0, 0.0).astype(BF)

    for way in range(2):
        for c in range(TAPS):
            if way == 0:
                taps = [kernel_ref[(6 - a) * 7 + 6 - c : (6 - a) * 7 + 7 - c, :] for a in range(TAPS)]
            else:
                taps = [kernel_ref[a * 7 + c : a * 7 + c + 1, :] for a in range(TAPS)]
            values = leaf_weights(taps + [None])[:LEAVES]
            for leaf, value in enumerate(values):
                weights[way, leaf, c] = jnp.broadcast_to(value, (8, 512))

    cp_lat.wait()

    @pl.loop(0, 8)
    def _(i):
        feats_copy(i).wait()
        rows = pl.ds(pl.multiple_of(i * chunk_rows, chunk_rows), chunk_rows)
        block = jnp.dot(feats[rows, :], lateral[...], preferred_element_type=F32).astype(BF)
        block = block.reshape(2, 128, 512)
        proj[i // 4, pl.ds(lax.rem(i, 4) * 2, 2)] = block

    cp_grad.wait()

    @pl.loop(0, 16)
    def _(i):
        own_g[i] = jnp.dot(spread, grad[i // 8, lax.rem(i, 8)], preferred_element_type=F32)

    def stencil(way, k, halo, own, store):
        tile = lax.rem(k, 2)
        lanes = pl.ds(pl.multiple_of((k // 2) * 128, 128), 128)
        for side in range(2):
            inside = s > 0 if side == 0 else s < n_s - 1
            for i in range(3):
                x = jnp.dot(spread, halo[side, tile, i, :, lanes], preferred_element_type=F32)
                rims[side * 3 + i] = jnp.where(inside, x, 0.0)

        @pl.loop(0, EXT // 16)
        def _(j):
            at = pl.ds(pl.multiple_of(j * 16, 16), 16)
            values = [rims[i, at, :] for i in range(3)]
            values += [own[tile * 8 + i, at, lanes] for i in range(8)]
            values += [rims[3 + i, at, :] for i in range(3)]
            for leaf, value in enumerate(leaf_inputs(values + [None])[:LEAVES]):
                leaf_u[leaf, at, :] = value

        @pl.loop(0, LEAVES // 2)
        def _(pair):
            for leaf in (pair * 2, pair * 2 + 1):
                u = leaf_u[leaf].reshape(SEG + 2 * HALF, 8, 128)
                total = None
                for c in range(TAPS):
                    term = weights[way, leaf, c, :, lanes][None] * u[c : c + SEG]
                    total = term if total is None else total + term
                leaf_v[leaf] = total.reshape(128, 128)

        @pl.loop(0, 8)
        def _(j):
            at = pl.ds(pl.multiple_of(j * 16, 16), 16)
            values = [leaf_v[leaf, at, :] for leaf in range(LEAVES)]
            for i, value in enumerate(leaf_outputs(values + [None])):
                store(tile, lanes, i, at, value.astype(BF))

    def to_pieces(tile, lanes, i, at, value):
        pieces[i, at, :] = value

    def to_sm(tile, lanes, i, at, value):
        sm[tile, i, at, lanes] = value

    @pl.loop(0, PIECES)
    def _(k):
        rim_wait(0, k)

        @pl.when(k + WINDOW < PIECES)
        def _():
            rim_start(0, k + WINDOW)

        @pl.when(k + WINDOW >= PIECES)
        def _():
            rim_start(1, k + WINDOW - PIECES)

        stencil(0, k, halo_g, own_g, to_pieces)
        tile = lax.rem(k, 2)
        lanes = pl.ds(pl.multiple_of((k // 2) * 128, 128), 128)
        for i in range(8):
            gp[tile, i, :, lanes] = jnp.dot(gather, pieces[i], preferred_element_type=F32).astype(BF)

    cp_gp = pltpu.make_async_copy(gp, gp_h, out_sem.at[0])
    cp_gp.start()

    @pl.loop(0, 16)
    def _(i):
        own_p[i] = jnp.dot(spread, proj[i // 8, lax.rem(i, 8)], preferred_element_type=F32)

    q16 = stacked(jnp.transpose(q_ref[...]))
    gq = fold(nt(q16, gp[...].reshape(2048, 512)))
    left = fold(jnp.dot(stacked(gq), feats[...], preferred_element_type=F32))
    cp_err.wait()
    e_high, e_low = split(error[...])
    left = left + fold(nt(q16, e_high)) + fold(nt(q16, e_low))

    def reduce_all(value, blocks, size, buf, rs, part, everyone, out, base):
        buf[...] = jnp.zeros_like(buf)
        for b in range(blocks):
            buf[pl.ds(b, 8, stride=size), :] = value[:, b * 128 : (b + 1) * 128]

        def scatter(i):
            peer = lax.rem(d + i, n_d)
            return pltpu.make_async_remote_copy(
                src_ref=buf.at[pl.ds(pl.multiple_of(peer * size, size), size)],
                dst_ref=rs.at[i - 1],
                send_sem=send1.at[base, i - 1], recv_sem=recv1.at[base, i - 1],
                device_id={"dp": peer}, device_id_type=MESH,
            )

        def across(i):
            return pltpu.make_async_remote_copy(
                src_ref=part, dst_ref=everyone.at[s],
                send_sem=send2.at[base, i - 1], recv_sem=recv2.at[base, i - 1],
                device_id={"space": lax.rem(s + i, n_s)}, device_id_type=MESH,
            )

        mine = pl.ds(pl.multiple_of(d * size, size), size)

        def around(i):
            return pltpu.make_async_remote_copy(
                src_ref=out.at[mine], dst_ref=out.at[mine],
                send_sem=send3.at[base, i - 1], recv_sem=recv3.at[base, i - 1],
                device_id={"dp": lax.rem(d + i, n_d)}, device_id_type=MESH,
            )

        def step1():
            for i in range(1, n_d):
                scatter(i).start()

        def step2():
            for i in range(1, n_d):
                scatter(i).wait()
            total = buf[mine, :]
            for i in range(1, n_d):
                total = total + rs[i - 1]
            part[...] = total
            everyone[s] = total
            for i in range(1, n_s):
                across(i).start()

        def step3():
            for i in range(1, n_s):
                across(i).wait()
            total = everyone[0]
            for i in range(1, n_s):
                total = total + everyone[i]
            out[mine, :] = total * (1.0 / (n_s * n_d))
            for i in range(1, n_d):
                around(i).start()

        def step4():
            for i in range(1, n_d):
                around(i).wait()
            return [out[pl.ds(b, 8, stride=size), :] for b in range(blocks)]

        return step1, step2, step3, step4

    def forward(first, last):
        @pl.loop(first, last)
        def _(k):
            rim_wait(1, k)

            @pl.when(k + WINDOW < PIECES)
            def _():
                rim_start(1, k + WINDOW)

            stencil(1, k, halo_p, own_p, to_sm)

    steps = reduce_all(left, 12, 16, p_buf, p_rs, p_part, p_all, p_out, 0)
    steps[0]()
    forward(0, 1)
    steps[1]()
    forward(1, 2)
    steps[2]()
    forward(2, 3)
    columns = steps[3]()

    at_row = lax.broadcasted_iota(jnp.int32, (8, 128), 0)
    for i in range(8):
        total = None
        lead = [x[i : i + 1, :] for x in columns]
        for x, y in zip(columns, lead):
            total = x * y if total is None else total + x * y
        dots = jnp.sum(total, axis=1, keepdims=True)
        scale = 1.0 / jnp.sqrt(dots[i : i + 1, :] + 1e-06)
        take = jnp.where(at_row[:, :1] > i, dots * scale, 0.0)
        lead = [y * scale for y in lead]
        columns = [jnp.where(at_row == i, y, x - take * y) for x, y in zip(columns, lead)]
    basis = jnp.concatenate(columns, axis=1)
    basis_ref[...] = basis

    b16 = stacked(basis)
    z = fold(nt(b16, feats[...]))
    right = fold(jnp.dot(stacked(z), gp[...].reshape(2048, 512), preferred_element_type=F32))
    e_high, e_low = split(error[...])
    right = right + fold(jnp.dot(b16, e_high, preferred_element_type=F32))
    right = right + fold(jnp.dot(b16, e_low, preferred_element_type=F32))
    steps = reduce_all(right, 4, 8, r_buf, r_rs, r_part, r_all, r_out, 1)
    steps[0]()
    forward(3, 4)
    steps[1]()
    forward(4, 5)
    steps[2]()
    forward(5, 8)
    qt_ref[...] = jnp.concatenate(steps[3](), axis=1)
    cp_sm = pltpu.make_async_copy(sm, sm_h, out_sem.at[1])
    cp_sm.start()
    cp_gp.wait()
    cp_sm.wait()


def final_kernel(feats, gp_all, gp, lateral, sm, error, basis, qt, smoothed, grad_feats, q_next, update, error_next, scratch):
    step = pl.program_id(0)
    grad_feats[...] = nt(gp[...], lateral[...]).astype(BF)
    row = lax.broadcasted_iota(jnp.int32, (128, 128), 0)
    col = lax.broadcasted_iota(jnp.int32, (128, 128), 1)
    gather = jnp.where((col % 8) * SEG + col // 8 == row, 1.0, 0.0).astype(BF)
    for i in range(4):
        smoothed[i] = jnp.dot(gather, sm[i], preferred_element_type=F32).astype(BF)
    tn = (((0,), (0,)), ((), ()))
    b, q = basis[...], qt[...]
    full = lax.dot_general(b, q, tn, precision=lax.Precision.HIGHEST, preferred_element_type=F32)
    matrix = lax.dot_general(feats[...], gp_all[...], tn, preferred_element_type=F32)
    error_next[...] = matrix + error[...] - full
    s = lax.axis_index("space")

    @pl.when(step == s // 4)
    def _():
        scratch[...] = full
        update[...] = scratch[pl.ds(pl.multiple_of(lax.rem(s, 4) * 96, 8), 96), :]

    @pl.when(step == 0)
    def _():
        q_next[...] = jnp.transpose(q)


def body(feats, lateral, kernel, grad_out, error, q_prev):
    flat = feats.reshape(2048, 1536)
    dma = pltpu.SemaphoreType.DMA
    anywhere = pl.BlockSpec(memory_space=pl.ANY)
    vmem = pl.BlockSpec(memory_space=pltpu.VMEM)
    gp, sm, basis, qt = pl.pallas_call(
        main_kernel,
        out_shape=(
            jax.ShapeDtypeStruct((2, 8, 128, 512), BF),
            jax.ShapeDtypeStruct((2, 8, 128, 512), BF),
            jax.ShapeDtypeStruct((8, 1536), F32),
            jax.ShapeDtypeStruct((8, 512), F32),
        ),
        in_specs=[anywhere] * 4 + [vmem] * 2,
        out_specs=(anywhere, anywhere, vmem, vmem),
        scratch_shapes=[
            pltpu.VMEM((2048, 1536), BF),
            pltpu.VMEM((1536, 512), BF),
            pltpu.VMEM((2, 8, 128, 512), BF),
            pltpu.VMEM((1536, 512), F32),
            pltpu.VMEM((2, 8, 128, 512), BF),
            pltpu.VMEM((2, 8, 128, 512), BF),
            pltpu.VMEM((2, 8, 128, 512), BF),
            pltpu.VMEM((2, 2, 3, 128, 512), BF),
            pltpu.VMEM((2, 2, 3, 128, 512), BF),
            pltpu.VMEM((16, EXT, 512), F32),
            pltpu.VMEM((16, EXT, 512), F32),
            pltpu.VMEM((6, EXT, 128), F32),
            pltpu.VMEM((LEAVES, EXT, 128), F32),
            pltpu.VMEM((LEAVES, 128, 128), F32),
            pltpu.VMEM((2, LEAVES, TAPS, 8, 512), F32),
            pltpu.VMEM((8, 128, 128), BF),
            pltpu.VMEM((128, 128), F32),
            pltpu.VMEM((7, 16, 128), F32),
            pltpu.VMEM((16, 128), F32),
            pltpu.VMEM((16, 16, 128), F32),
            pltpu.VMEM((128, 128), F32),
            pltpu.VMEM((64, 128), F32),
            pltpu.VMEM((7, 8, 128), F32),
            pltpu.VMEM((8, 128), F32),
            pltpu.VMEM((16, 8, 128), F32),
            pltpu.VMEM((64, 128), F32),
            dma((3,)),
            dma((8,)),
            dma((2,)),
            dma((32,)),
            dma((32,)),
            dma((2, 7)),
            dma((2, 7)),
            dma((2, 15)),
            dma((2, 15)),
            dma((2, 7)),
            dma((2, 7)),
        ],
        compiler_params=pltpu.CompilerParams(
            collective_id=0, has_side_effects=True, vmem_limit_bytes=60 * 2**20
        ),
        name="exchange",
    )(flat, lateral, grad_out, error, kernel.reshape(49, 512), q_prev)

    rows = gp.reshape(2048, 512)
    whole = lambda *shape: pl.BlockSpec(shape, lambda i: (0,) * len(shape))
    smoothed, grad_feats, q_next, update, error_next = pl.pallas_call(
        final_kernel,
        grid=(4,),
        out_shape=(
            jax.ShapeDtypeStruct((16, 128, 512), BF),
            jax.ShapeDtypeStruct((2048, 1536), BF),
            jax.ShapeDtypeStruct((512, 8), F32),
            jax.ShapeDtypeStruct((96, 512), F32),
            jax.ShapeDtypeStruct((1536, 512), F32),
        ),
        in_specs=[
            pl.BlockSpec((2048, 384), lambda i: (0, i)),
            whole(2048, 512),
            pl.BlockSpec((512, 512), lambda i: (i, 0)),
            whole(1536, 512),
            pl.BlockSpec((4, 128, 512), lambda i: (i, 0, 0)),
            pl.BlockSpec((384, 512), lambda i: (i, 0)),
            pl.BlockSpec((8, 384), lambda i: (0, i)),
            whole(8, 512),
        ],
        out_specs=(
            pl.BlockSpec((4, 128, 512), lambda i: (i, 0, 0)),
            pl.BlockSpec((512, 1536), lambda i: (i, 0)),
            whole(512, 8),
            whole(96, 512),
            pl.BlockSpec((384, 512), lambda i: (i, 0)),
        ),
        scratch_shapes=[pltpu.VMEM((384, 512), F32)],
        compiler_params=pltpu.CompilerParams(vmem_limit_bytes=56 * 2**20),
        name="finish",
    )(flat, rows, rows, lateral, sm.reshape(16, 128, 512), error, basis, qt)
    return (
        smoothed.reshape(2, 8, 128, 512),
        grad_feats.reshape(2, 8, 128, 1536),
        q_next,
        update,
        error_next,
    )


def solution(mesh):
    placed = (
        P("dp", "space", None, None),
        P(),
        P(),
        P("dp", "space", None, None),
        P(("dp", "space"), None),
        P(),
    )
    return jax.shard_map(
        body,
        mesh=mesh,
        in_specs=placed,
        out_specs=(
            P("dp", "space", None, None),
            P("dp", "space", None, None),
            P(),
            P("space", None),
            P(("dp", "space"), None),
        ),
        check_vma=False,
    )
```

```python
import jax
import jax.numpy as jnp
from jax import lax
from jax.experimental import pallas as pl
from jax.experimental.pallas import tpu as pltpu
from jax.sharding import PartitionSpec as P

MESH = pl.DeviceIdType.MESH
BF = jnp.bfloat16
F32 = jnp.float32
TAPS = 7
HALF = 3
LEAVES = 26
EXT = 144
PIECES = 8
GROUP = 13


def leaf_inputs(d):
    if len(d) == 1:
        return [d[0]]
    size = (len(d) + 1) // 2
    half, span = size // 2, size - 1
    sub = lambda x, y: None if x is None or y is None else x - y
    d0, d1, d2 = d[:span], d[half : half + span], d[size : size + span]
    first = [sub(x, y) for x, y in zip(d0, d1)]
    last = [sub(x, y) for x, y in zip(d2, d1)]
    return leaf_inputs(first) + leaf_inputs(d1) + leaf_inputs(last)


def leaf_weights(h):
    if len(h) == 1:
        return [h[0]]
    half = len(h) // 2
    low, high = h[:half], h[half:]
    both = [x if y is None else x + y for x, y in zip(low, high)]
    return leaf_weights(low) + leaf_weights(both) + leaf_weights(high)


def leaf_outputs(m):
    if len(m) == 1:
        return [m[0]]
    third = len(m) // 3
    first, mid, last = (leaf_outputs(m[i * third : (i + 1) * third]) for i in range(3))
    add = lambda x, y: x if y is None else x + y
    return [add(y, x) for x, y in zip(first, mid)] + [add(x, y) for x, y in zip(mid, last)]


def split(x):
    high = x.astype(BF)
    return high, (x - high.astype(F32)).astype(BF)


def stacked(x):
    high = x.astype(BF).astype(F32)
    return jnp.concatenate([high, x - high], axis=0).astype(BF)


def nt(x, y):
    return lax.dot_general(x, y, (((1,), (1,)), ((), ())), preferred_element_type=F32)


def fold(x):
    return x[:8] + x[8:16]


def main_kernel(
    feats_h, lateral_h, grad_h, error_h, kernel_ref, q_ref,
    gp, sm, matrix, lateral, basis_ref, qt_ref,
    feats, grad, error, proj, halo_g, halo_p, leaf_u, leaf_v, weights, taps_q, spread_q, own_h, far_h,
    p_buf, p_rs, p_part, p_all, p_out, r_buf, r_rs, r_part, r_all, r_out,
    in_sem, feats_sem, halo_send, halo_recv, h_send, h_recv, send1, recv1, send2, recv2, send3, recv3,
):
    s, d = lax.axis_index("space"), lax.axis_index("dp")
    n_s, n_d = 16, 8
    up, down = lax.rem(s + 1, n_s), lax.rem(s + n_s - 1, n_s)
    chunk_rows = 256

    cp_grad = pltpu.make_async_copy(grad_h, grad, in_sem.at[0])
    cp_lat = pltpu.make_async_copy(lateral_h, lateral, in_sem.at[1])
    cp_err = pltpu.make_async_copy(error_h, error, in_sem.at[2])
    cp_grad.start()
    cp_lat.start()

    def feats_copy(i):
        rows = pl.ds(pl.multiple_of(i * chunk_rows, chunk_rows), chunk_rows)
        return pltpu.make_async_copy(feats_h.at[rows], feats.at[rows], feats_sem.at[i])

    @pl.loop(0, 8)
    def _(i):
        feats_copy(i).start()

    cp_err.start()

    barrier = pltpu.get_barrier_semaphore()

    place_x, place_y = s // 4, lax.rem(s, 4)

    def along(axis, i):
        if axis == 0:
            return lax.rem(place_x + i, 4) * 4 + place_y
        return place_x * 4 + lax.rem(place_y + i, 4)

    def greet(**to):
        pl.semaphore_signal(barrier, inc=1, device_id=to, device_id_type=MESH)

    greet(space=up)
    greet(space=down)
    for i in range(1, 4):
        greet(space=along(1, i))
        greet(space=along(0, i))
    for i in range(1, n_d):
        greet(dp=lax.rem(d + i, n_d))
    pl.semaphore_wait(barrier, 2 + 6 + n_d - 1)

    def rim_copy(which, k, side):
        tile = lax.rem(k, 2)
        lanes = pl.ds(pl.multiple_of((k // 2) * 128, 128), 128)
        source, target = (grad_h, halo_g) if which == 0 else (proj, halo_p)
        rows = pl.ds(5, 3) if side == 0 else pl.ds(0, 3)
        at = (which * PIECES + k) * 2 + side
        return pltpu.make_async_remote_copy(
            src_ref=source.at[tile, rows, :, lanes],
            dst_ref=target.at[side, tile, :, :, lanes],
            send_sem=halo_send.at[at],
            recv_sem=halo_recv.at[at],
            device_id={"space": up if side == 0 else down},
            device_id_type=MESH,
        )

    def rim_start(which, k):
        rim_copy(which, k, 0).start()
        rim_copy(which, k, 1).start()

    def rim_wait(which, k):
        rim_copy(which, k, 0).wait()
        rim_copy(which, k, 1).wait()

    def rims_start(which, first, last):
        @pl.loop(first, last)
        def _(k):
            rim_start(which, k)

    rims_start(0, 0, 2)

    for way in range(2):
        for c in range(TAPS):
            if way == 0:
                taps = [kernel_ref[6 - a, 6 - c : 7 - c, :] for a in range(TAPS)]
            else:
                taps = [kernel_ref[a, c : c + 1, :] for a in range(TAPS)]
            values = leaf_weights(taps + [None])[:LEAVES]
            for leaf, value in enumerate(values):
                weights[way, leaf, c] = jnp.broadcast_to(value, (8, 512))

    leaf_u[:, :8, :] = jnp.zeros((LEAVES, 8, 128), F32)
    leaf_u[:, 136:, :] = jnp.zeros((LEAVES, 8, 128), F32)

    q8 = q_ref[...]
    for a in range(TAPS):
        for c in range(TAPS):
            term = kernel_ref[a, c : c + 1, :] * q8
            high = term.astype(BF).astype(F32)
            at = (a * TAPS + c) * 8
            taps_q[0, at : at + 8, :] = high
            taps_q[1, at : at + 8, :] = term - high
    taps_high, taps_low = taps_q[0].astype(BF), taps_q[1].astype(BF)
    cp_grad.wait()
    for i in range(8):
        cells = grad[i // 4, (i % 4) * 2 : (i % 4) * 2 + 2].reshape(256, 512)
        spread_q[:, i * 256 : (i + 1) * 256] = nt(taps_high, cells) + nt(taps_low, cells)
    lane = lax.broadcasted_iota(jnp.int32, (8, 128), 1)

    @pl.loop(0, 2)
    def _(tile):
        for o in range(14):
            total = None
            for c in range(TAPS):
                part = None
                for a in range(max(0, o - 7), min(TAPS, o + 1)):
                    at = (a * TAPS + c) * 8
                    x = spread_q[at : at + 8, pl.ds(pl.multiple_of(tile * 1024 + (o - a) * 128, 128), 128)]
                    part = x if part is None else part + x
                shift = c - HALF
                if shift > 0:
                    part = jnp.where(lane >= shift, pltpu.roll(part, shift, 1), 0.0)
                if shift < 0:
                    part = jnp.where(lane < 128 + shift, pltpu.roll(part, 128 + shift, 1), 0.0)
                total = part if total is None else total + part
            own_h[tile, o] = total

    def h_copy(side):
        return pltpu.make_async_remote_copy(
            src_ref=own_h.at[:, pl.ds(11, 3)] if side == 0 else own_h.at[:, pl.ds(0, 3)],
            dst_ref=far_h.at[side],
            send_sem=h_send.at[side], recv_sem=h_recv.at[side],
            device_id={"space": up if side == 0 else down}, device_id_type=MESH,
        )

    h_copy(0).start()
    h_copy(1).start()
    rims_start(0, 2, 3)

    q16 = stacked(q8)
    cp_err.wait()
    e_high, e_low = split(error[...])
    left = fold(nt(q16, e_high)) + fold(nt(q16, e_low))
    cp_lat.wait()

    def project(first, last):
        @pl.loop(first, last)
        def _(i):
            rows = pl.ds(pl.multiple_of(i * chunk_rows, chunk_rows), chunk_rows)
            block = jnp.dot(feats[rows, :], lateral[...], preferred_element_type=F32).astype(BF)
            proj[i // 4, pl.ds(lax.rem(i, 4) * 2, 2)] = block.reshape(2, 128, 512)

    @pl.loop(0, 8)
    def _(i):
        feats_copy(i).wait()

    def stencil(way, k, halo, own, out):
        tile = lax.rem(k, 2)
        lanes = pl.ds(pl.multiple_of((k // 2) * 128, 128), 128)

        @pl.loop(0, 8, unroll=2)
        def _(j):
            at = pl.ds(pl.multiple_of(j * 16, 16), 16)
            values = [jnp.where(s > 0, halo[0, tile, i, at, lanes].astype(F32), 0.0) for i in range(3)]
            values += [own[tile, i, at, lanes].astype(F32) for i in range(8)]
            values += [jnp.where(s < n_s - 1, halo[1, tile, i, at, lanes].astype(F32), 0.0) for i in range(3)]
            to = pl.ds(pl.multiple_of(j * 16 + 8, 8), 16)
            for leaf, value in enumerate(leaf_inputs(values + [None])[:LEAVES]):
                leaf_u[leaf, to, :] = value

        @pl.loop(0, LEAVES // GROUP)
        def _(group):
            for place in range(GROUP):
                leaf = group * GROUP + place
                taps = [weights[way, leaf, c, :, lanes] for c in range(TAPS)]
                for b in range(16):
                    total = None
                    for c in range(TAPS):
                        term = taps[c] * leaf_u[leaf, pl.ds(8 * b + 8 - HALF + c, 8), :]
                        total = term if total is None else total + term
                    leaf_v[leaf, 8 * b : 8 * b + 8, :] = total

        @pl.loop(0, 8, unroll=2)
        def _(j):
            at = pl.ds(pl.multiple_of(j * 16, 16), 16)
            values = [leaf_v[leaf, at, :] for leaf in range(LEAVES)]
            for i, value in enumerate(leaf_outputs(values + [None])):
                out[tile, i, at, lanes] = value.astype(BF)

    def backward(first, last):
        @pl.loop(first, last)
        def _(k):
            rim_wait(0, k)

            stencil(0, k, halo_g, grad, gp)

    h_copy(0).wait()
    h_copy(1).wait()
    places = []
    for tile in range(2):
        for i in range(8):
            x = own_h[tile, i + HALF]
            if i < HALF:
                x = x + jnp.where(s > 0, far_h[0, tile, i], 0.0)
            if i >= 8 - HALF:
                x = x + jnp.where(s < n_s - 1, far_h[1, tile, i - 8 + HALF], 0.0)
            places.append(x)
    gq = stacked(jnp.concatenate(places, axis=1))
    left = left + fold(jnp.dot(gq, feats[...], preferred_element_type=F32))

    def reduce_all(value, blocks, size, buf, rs, part, lines, out, base):
        buf[...] = jnp.zeros_like(buf)
        for b in range(blocks):
            buf[pl.ds(b, 8, stride=size), :] = value[:, b * 128 : (b + 1) * 128]

        def scatter(i):
            peer = lax.rem(d + i, n_d)
            return pltpu.make_async_remote_copy(
                src_ref=buf.at[pl.ds(pl.multiple_of(peer * size, size), size)],
                dst_ref=rs.at[i - 1],
                send_sem=send1.at[base, i - 1], recv_sem=recv1.at[base, i - 1],
                device_id={"dp": peer}, device_id_type=MESH,
            )

        def across(axis, i):
            at = axis * 3 + i - 1
            return pltpu.make_async_remote_copy(
                src_ref=part.at[axis], dst_ref=lines.at[axis, place_y if axis else place_x],
                send_sem=send2.at[base, at], recv_sem=recv2.at[base, at],
                device_id={"space": along(axis, i)}, device_id_type=MESH,
            )

        def line_start(axis, total):
            part[axis] = total
            lines[axis, place_y if axis else place_x] = total
            for i in range(1, 4):
                across(axis, i).start()

        def line_sum(axis):
            for i in range(1, 4):
                across(axis, i).wait()
            return (lines[axis, 0] + lines[axis, 1]) + (lines[axis, 2] + lines[axis, 3])

        mine = pl.ds(pl.multiple_of(d * size, size), size)

        def around(i):
            return pltpu.make_async_remote_copy(
                src_ref=out.at[mine], dst_ref=out.at[mine],
                send_sem=send3.at[base, i - 1], recv_sem=recv3.at[base, i - 1],
                device_id={"dp": lax.rem(d + i, n_d)}, device_id_type=MESH,
            )

        def step1():
            for i in range(1, n_d):
                scatter(i).start()

        def step2():
            for i in range(1, n_d):
                scatter(i).wait()
            total = buf[mine, :]
            for i in range(1, n_d):
                total = total + rs[i - 1]
            line_start(0, total)

        def step3():
            line_start(1, line_sum(0))

        def step4():
            out[mine, :] = line_sum(1) * (1.0 / (n_s * n_d))
            for i in range(1, n_d):
                around(i).start()

        def step5():
            for i in range(1, n_d):
                around(i).wait()
            return [out[pl.ds(b, 8, stride=size), :] for b in range(blocks)]

        return step1, step2, step3, step4, step5

    def forward(first, last):
        @pl.loop(first, last)
        def _(k):
            rim_wait(1, k)

            stencil(1, k, halo_p, proj, sm)

    steps = reduce_all(left, 12, 16, p_buf, p_rs, p_part, p_all, p_out, 0)
    steps[0]()
    rims_start(0, 3, 4)
    project(0, 4)
    rims_start(0, 4, 5)
    project(4, 8)
    steps[1]()
    rims_start(0, 5, 6)
    backward(0, 2)
    steps[2]()
    rims_start(0, 6, 8)
    backward(2, 5)
    steps[3]()
    rims_start(1, 0, 1)
    backward(5, 7)
    rims_start(1, 1, 2)
    backward(7, 8)
    columns = steps[4]()

    at_row = lax.broadcasted_iota(jnp.int32, (8, 128), 0)
    for i in range(8):
        total = None
        lead = [x[i : i + 1, :] for x in columns]
        for x, y in zip(columns, lead):
            total = x * y if total is None else total + x * y
        dots = jnp.sum(total, axis=1, keepdims=True)
        scale = 1.0 / jnp.sqrt(dots[i : i + 1, :] + 1e-06)
        take = jnp.where(at_row[:, :1] > i, dots * scale, 0.0)
        lead = [y * scale for y in lead]
        columns = [jnp.where(at_row == i, y, x - take * y) for x, y in zip(columns, lead)]
    basis = jnp.concatenate(columns, axis=1)
    basis_ref[...] = basis

    rims_start(1, 2, 3)
    b16 = stacked(basis)
    z = fold(nt(b16, feats[...]))
    right = fold(jnp.dot(stacked(z), gp[...].reshape(2048, 512), preferred_element_type=F32))
    e_high, e_low = split(error[...])
    right = right + fold(jnp.dot(b16, e_high, preferred_element_type=F32))
    right = right + fold(jnp.dot(b16, e_low, preferred_element_type=F32))
    steps = reduce_all(right, 4, 8, r_buf, r_rs, r_part, r_all, r_out, 1)
    steps[0]()

    def gradient(first, last):
        @pl.loop(first, last)
        def _(i):
            at = pl.ds(pl.multiple_of(i * 256, 256), 256)
            tn = (((0,), (0,)), ((), ()))
            block = lax.dot_general(feats[:, at], gp[...].reshape(2048, 512), tn, preferred_element_type=F32)
            matrix[at, :] = block + error[at, :]

    rims_start(1, 3, 4)
    gradient(0, 4)
    forward(0, 1)
    steps[1]()
    rims_start(1, 4, 6)
    forward(1, 3)
    gradient(4, 6)
    steps[2]()
    rims_start(1, 6, 8)
    forward(3, 5)
    steps[3]()
    forward(5, 7)
    qt_ref[...] = jnp.concatenate(steps[4](), axis=1)
    forward(7, 8)


def final_kernel(
    gp, sm, matrix, lateral, basis, qt,
    smoothed, grad_feats, q_next, update, error_next,
    feats_v, error_v, full_v, small_sem, feats_sem, error_sem,
):
    cp_sm = pltpu.make_async_copy(sm, smoothed, small_sem.at[0])
    cp_sm.start()
    b, q = basis[...], qt[...]
    b_high, q_high = b.astype(BF).astype(F32), q.astype(BF).astype(F32)
    b24 = jnp.concatenate([b_high, b - b_high, b_high], axis=0).astype(BF)
    q24 = jnp.concatenate([q_high, q_high, q - q_high], axis=0).astype(BF)
    q_next[...] = q
    s = lax.axis_index("space")
    tn = (((0,), (0,)), ((), ()))

    def feats_copy(i):
        rows = pl.ds(i * 256, 256)
        return pltpu.make_async_copy(feats_v.at[rows], grad_feats.at[rows], feats_sem.at[i])

    def error_copy(i):
        rows = pl.ds(i * 384, 384)
        return pltpu.make_async_copy(error_v.at[rows], error_next.at[rows], error_sem.at[i])

    for i in range(8):
        cells = gp[i // 4, (i % 4) * 2 : (i % 4) * 2 + 2].reshape(256, 512)
        feats_v[i * 256 : (i + 1) * 256, :] = nt(cells, lateral[...]).astype(BF)
        feats_copy(i).start()
        if i % 2 == 0:
            j = i // 2
            full = lax.dot_general(b24[:, j * 384 : (j + 1) * 384], q24, tn, preferred_element_type=F32)
            rows = slice(j * 384, (j + 1) * 384)
            error_v[rows, :] = matrix[rows, :] - full
            error_copy(j).start()

            @pl.when(s // 4 == j)
            def _():
                full_v[...] = full

    update[...] = full_v[pl.ds(pl.multiple_of(lax.rem(s, 4) * 96, 8), 96), :]
    cp_sm.wait()
    for i in range(8):
        feats_copy(i).wait()
    for i in range(4):
        error_copy(i).wait()


def body(feats, lateral, kernel, grad_out, error, q_prev):
    dma = pltpu.SemaphoreType.DMA
    hbm = pl.BlockSpec(memory_space=pltpu.HBM)
    vmem = pl.BlockSpec(memory_space=pltpu.VMEM)
    gp, sm, matrix, weight, basis, qt = pl.pallas_call(
        main_kernel,
        out_shape=(
            pltpu.VMEM((2, 8, 128, 512), BF),
            pltpu.VMEM((2, 8, 128, 512), BF),
            pltpu.VMEM((1536, 512), F32),
            pltpu.VMEM((1536, 512), BF),
            pltpu.VMEM((8, 1536), F32),
            pltpu.VMEM((8, 512), F32),
        ),
        in_specs=[hbm] * 4 + [vmem] * 2,
        out_specs=(vmem,) * 6,
        scratch_shapes=[
            pltpu.VMEM((2048, 1536), BF),
            pltpu.VMEM((2, 8, 128, 512), BF),
            pltpu.VMEM((1536, 512), F32),
            pltpu.VMEM((2, 8, 128, 512), BF),
            pltpu.VMEM((2, 2, 3, 128, 512), BF),
            pltpu.VMEM((2, 2, 3, 128, 512), BF),
            pltpu.VMEM((LEAVES, EXT, 128), F32),
            pltpu.VMEM((LEAVES, 128, 128), F32),
            pltpu.VMEM((2, LEAVES, TAPS, 8, 512), F32),
            pltpu.VMEM((2, 392, 512), F32),
            pltpu.VMEM((392, 2048), F32),
            pltpu.VMEM((2, 14, 8, 128), F32),
            pltpu.VMEM((2, 2, 3, 8, 128), F32),
            pltpu.VMEM((128, 128), F32),
            pltpu.VMEM((7, 16, 128), F32),
            pltpu.VMEM((2, 16, 128), F32),
            pltpu.VMEM((2, 4, 16, 128), F32),
            pltpu.VMEM((128, 128), F32),
            pltpu.VMEM((64, 128), F32),
            pltpu.VMEM((7, 8, 128), F32),
            pltpu.VMEM((2, 8, 128), F32),
            pltpu.VMEM((2, 4, 8, 128), F32),
            pltpu.VMEM((64, 128), F32),
            dma((3,)),
            dma((8,)),
            dma((32,)),
            dma((32,)),
            dma((2,)),
            dma((2,)),
            dma((2, 7)),
            dma((2, 7)),
            dma((2, 6)),
            dma((2, 6)),
            dma((2, 7)),
            dma((2, 7)),
        ],
        compiler_params=pltpu.CompilerParams(
            collective_id=0, has_side_effects=True, vmem_limit_bytes=46 * 2**20
        ),
        name="exchange",
    )(feats.reshape(2048, 1536), lateral, grad_out, error, kernel, q_prev.T)

    smoothed, grad_feats, q_next, update, error_next = pl.pallas_call(
        final_kernel,
        out_shape=(
            jax.ShapeDtypeStruct((2, 8, 128, 512), BF),
            jax.ShapeDtypeStruct((2048, 1536), BF),
            jax.ShapeDtypeStruct((8, 512), F32),
            jax.ShapeDtypeStruct((96, 512), F32),
            jax.ShapeDtypeStruct((1536, 512), F32),
        ),
        in_specs=[vmem] * 6,
        out_specs=(hbm, hbm, vmem, vmem, hbm),
        scratch_shapes=[
            pltpu.VMEM((2048, 1536), BF),
            pltpu.VMEM((1536, 512), F32),
            pltpu.VMEM((384, 512), F32),
            dma((1,)),
            dma((8,)),
            dma((4,)),
        ],
        compiler_params=pltpu.CompilerParams(vmem_limit_bytes=24 * 2**20),
        name="finish",
    )(gp, sm, matrix, weight, basis, qt)
    return smoothed, grad_feats.reshape(2, 8, 128, 1536), q_next.T, update, error_next


def solution(mesh):
    placed = (
        P("dp", "space", None, None),
        P(),
        P(),
        P("dp", "space", None, None),
        P(("dp", "space"), None),
        P(),
    )
    return jax.shard_map(
        body,
        mesh=mesh,
        in_specs=placed,
        out_specs=(
            P("dp", "space", None, None),
            P("dp", "space", None, None),
            P(),
            P("space", None),
            P(("dp", "space"), None),
        ),
        check_vma=False,
    )
```

```python
import jax
import jax.numpy as jnp
from jax import lax
from jax.experimental import pallas as pl
from jax.experimental.pallas import tpu as pltpu
from jax.sharding import PartitionSpec as P

MESH = pl.DeviceIdType.MESH
BF = jnp.bfloat16
F32 = jnp.float32
TAPS = 7
HALF = 3
LEAVES = 26
EXT = 144
PIECES = 8
GROUP = 13


def leaf_inputs(d):
    if len(d) == 1:
        return [d[0]]
    size = (len(d) + 1) // 2
    half, span = size // 2, size - 1
    sub = lambda x, y: None if x is None or y is None else x - y
    d0, d1, d2 = d[:span], d[half : half + span], d[size : size + span]
    first = [sub(x, y) for x, y in zip(d0, d1)]
    last = [sub(x, y) for x, y in zip(d2, d1)]
    return leaf_inputs(first) + leaf_inputs(d1) + leaf_inputs(last)


def leaf_weights(h):
    if len(h) == 1:
        return [h[0]]
    half = len(h) // 2
    low, high = h[:half], h[half:]
    both = [x if y is None else x + y for x, y in zip(low, high)]
    return leaf_weights(low) + leaf_weights(both) + leaf_weights(high)


def leaf_outputs(m):
    if len(m) == 1:
        return [m[0]]
    third = len(m) // 3
    first, mid, last = (leaf_outputs(m[i * third : (i + 1) * third]) for i in range(3))
    add = lambda x, y: x if y is None else x + y
    return [add(y, x) for x, y in zip(first, mid)] + [add(x, y) for x, y in zip(mid, last)]


def split(x):
    high = x.astype(BF)
    return high, (x - high.astype(F32)).astype(BF)


def stacked(x):
    high = x.astype(BF).astype(F32)
    return jnp.concatenate([high, x - high], axis=0).astype(BF)


def nt(x, y):
    return lax.dot_general(x, y, (((1,), (1,)), ((), ())), preferred_element_type=F32)


def fold(x):
    return x[:8] + x[8:16]


def main_kernel(
    feats_h, lateral_h, grad_h, error_h, kernel_ref, q_ref,
    gp, sm, matrix, lateral, basis_ref, qt_ref,
    error_high, error_low, feats, grad, error, proj, halo_g, halo_p, leaf_u, leaf_v, weights, taps_q, spread_q, own_h, far_h,
    p_buf, p_rs, p_part, p_all, p_out, r_buf, r_rs, r_part, r_all, r_out,
    in_sem, feats_sem, halo_send, halo_recv, h_send, h_recv, send1, recv1, send2, recv2, send3, recv3,
):
    s, d = lax.axis_index("space"), lax.axis_index("dp")
    n_s, n_d = 16, 8
    up, down = lax.rem(s + 1, n_s), lax.rem(s + n_s - 1, n_s)
    chunk_rows = 256

    cp_grad = pltpu.make_async_copy(grad_h, grad, in_sem.at[0])
    cp_lat = pltpu.make_async_copy(lateral_h, lateral, in_sem.at[1])
    cp_err = pltpu.make_async_copy(error_h, error, in_sem.at[2])
    cp_grad.start()
    cp_lat.start()

    def feats_copy(i):
        rows = pl.ds(pl.multiple_of(i * chunk_rows, chunk_rows), chunk_rows)
        return pltpu.make_async_copy(feats_h.at[rows], feats.at[rows], feats_sem.at[i])

    @pl.loop(0, 8)
    def _(i):
        feats_copy(i).start()

    cp_err.start()

    barrier = pltpu.get_barrier_semaphore()

    place_x, place_y = s // 4, lax.rem(s, 4)

    def along(axis, i):
        if axis == 0:
            return lax.rem(place_x + i, 4) * 4 + place_y
        return place_x * 4 + lax.rem(place_y + i, 4)

    def greet(**to):
        pl.semaphore_signal(barrier, inc=1, device_id=to, device_id_type=MESH)

    greet(space=up)
    greet(space=down)
    for i in range(1, 4):
        greet(space=along(1, i))
        greet(space=along(0, i))
    for i in range(1, n_d):
        greet(dp=lax.rem(d + i, n_d))
    for way in range(2):
        for c in range(TAPS):
            if way == 0:
                taps = [kernel_ref[6 - a, 6 - c : 7 - c, :] for a in range(TAPS)]
            else:
                taps = [kernel_ref[a, c : c + 1, :] for a in range(TAPS)]
            values = leaf_weights(taps + [None])[:LEAVES]
            for leaf, value in enumerate(values):
                weights[way, leaf, c] = jnp.broadcast_to(value, (8, 512))

    leaf_u[:, :8, :] = jnp.zeros((LEAVES, 8, 128), F32)
    leaf_u[:, 136:, :] = jnp.zeros((LEAVES, 8, 128), F32)

    q8 = q_ref[...]
    for a in range(TAPS):
        for c in range(TAPS):
            term = kernel_ref[a, c : c + 1, :] * q8
            high = term.astype(BF).astype(F32)
            at = (a * TAPS + c) * 8
            taps_q[0, at : at + 8, :] = high
            taps_q[1, at : at + 8, :] = term - high
    pl.semaphore_wait(barrier, 2 + 6 + n_d - 1)

    def rim_copy(which, k, side):
        tile = lax.rem(k, 2)
        lanes = pl.ds(pl.multiple_of((k // 2) * 128, 128), 128)
        source, target = (grad_h, halo_g) if which == 0 else (proj, halo_p)
        rows = pl.ds(5, 3) if side == 0 else pl.ds(0, 3)
        at = (which * PIECES + k) * 2 + side
        return pltpu.make_async_remote_copy(
            src_ref=source.at[tile, rows, :, lanes],
            dst_ref=target.at[side, tile, :, :, lanes],
            send_sem=halo_send.at[at],
            recv_sem=halo_recv.at[at],
            device_id={"space": up if side == 0 else down},
            device_id_type=MESH,
        )

    def rim_start(which, k):
        rim_copy(which, k, 0).start()
        rim_copy(which, k, 1).start()

    def rim_wait(which, k):
        rim_copy(which, k, 0).wait()
        rim_copy(which, k, 1).wait()

    def rims_start(which, first, last):
        @pl.loop(first, last)
        def _(k):
            rim_start(which, k)

    rim_start(0, 0)

    taps_high, taps_low = taps_q[0].astype(BF), taps_q[1].astype(BF)
    cp_grad.wait()
    for i in range(8):
        cells = grad[i // 4, (i % 4) * 2 : (i % 4) * 2 + 2].reshape(256, 512)
        spread_q[:, i * 256 : (i + 1) * 256] = nt(taps_high, cells) + nt(taps_low, cells)
    lane = lax.broadcasted_iota(jnp.int32, (8, 128), 1)

    @pl.loop(0, 2)
    def _(tile):
        for o in range(14):
            total = None
            for c in range(TAPS):
                part = None
                for a in range(max(0, o - 7), min(TAPS, o + 1)):
                    at = (a * TAPS + c) * 8
                    x = spread_q[at : at + 8, pl.ds(pl.multiple_of(tile * 1024 + (o - a) * 128, 128), 128)]
                    part = x if part is None else part + x
                shift = c - HALF
                if shift > 0:
                    part = jnp.where(lane >= shift, pltpu.roll(part, shift, 1), 0.0)
                if shift < 0:
                    part = jnp.where(lane < 128 + shift, pltpu.roll(part, 128 + shift, 1), 0.0)
                total = part if total is None else total + part
            own_h[tile, o] = total

    def h_copy(side):
        return pltpu.make_async_remote_copy(
            src_ref=own_h.at[:, pl.ds(11, 3)] if side == 0 else own_h.at[:, pl.ds(0, 3)],
            dst_ref=far_h.at[side],
            send_sem=h_send.at[side], recv_sem=h_recv.at[side],
            device_id={"space": up if side == 0 else down}, device_id_type=MESH,
        )

    h_copy(0).start()
    h_copy(1).start()
    rims_start(0, 1, 3)

    q16 = stacked(q8)
    cp_err.wait()
    error_high[...], error_low[...] = split(error[...])
    left = fold(nt(q16, error_high[...])) + fold(nt(q16, error_low[...]))
    cp_lat.wait()

    def project(first, last):
        @pl.loop(first, last)
        def _(i):
            rows = pl.ds(pl.multiple_of(i * 1024, 1024), 1024)
            block = jnp.dot(feats[rows, :], lateral[...], preferred_element_type=F32).astype(BF)
            proj[i] = block.reshape(8, 128, 512)

    @pl.loop(0, 8)
    def _(i):
        feats_copy(i).wait()

    def stencil(way, k, halo, own, out):
        tile = lax.rem(k, 2)
        lanes = pl.ds(pl.multiple_of((k // 2) * 128, 128), 128)

        @pl.loop(0, 8, unroll=2)
        def _(j):
            at = pl.ds(pl.multiple_of(j * 16, 16), 16)
            values = [jnp.where(s > 0, halo[0, tile, i, at, lanes].astype(F32), 0.0) for i in range(3)]
            values += [own[tile, i, at, lanes].astype(F32) for i in range(8)]
            values += [jnp.where(s < n_s - 1, halo[1, tile, i, at, lanes].astype(F32), 0.0) for i in range(3)]
            to = pl.ds(pl.multiple_of(j * 16 + 8, 8), 16)
            for leaf, value in enumerate(leaf_inputs(values + [None])[:LEAVES]):
                leaf_u[leaf, to, :] = value

        @pl.loop(0, LEAVES // GROUP)
        def _(group):
            for place in range(GROUP):
                leaf = group * GROUP + place
                taps = [weights[way, leaf, c, :, lanes] for c in range(TAPS)]
                for b in range(16):
                    total = None
                    for c in range(TAPS):
                        term = taps[c] * leaf_u[leaf, pl.ds(8 * b + 8 - HALF + c, 8), :]
                        total = term if total is None else total + term
                    leaf_v[leaf, 8 * b : 8 * b + 8, :] = total

        @pl.loop(0, 8, unroll=2)
        def _(j):
            at = pl.ds(pl.multiple_of(j * 16, 16), 16)
            values = [leaf_v[leaf, at, :] for leaf in range(LEAVES)]
            for i, value in enumerate(leaf_outputs(values + [None])):
                out[tile, i, at, lanes] = value.astype(BF)

    def backward(first, last):
        @pl.loop(first, last)
        def _(k):
            rim_wait(0, k)

            stencil(0, k, halo_g, grad, gp)

    h_copy(0).wait()
    h_copy(1).wait()
    places = []
    for tile in range(2):
        for i in range(8):
            x = own_h[tile, i + HALF]
            if i < HALF:
                x = x + jnp.where(s > 0, far_h[0, tile, i], 0.0)
            if i >= 8 - HALF:
                x = x + jnp.where(s < n_s - 1, far_h[1, tile, i - 8 + HALF], 0.0)
            places.append(x)
    gq = stacked(jnp.concatenate(places, axis=1))
    left = left + fold(jnp.dot(gq, feats[...], preferred_element_type=F32))

    def reduce_all(value, blocks, size, buf, rs, part, lines, out, base):
        buf[...] = jnp.zeros_like(buf)
        for b in range(blocks):
            buf[pl.ds(b, 8, stride=size), :] = value[:, b * 128 : (b + 1) * 128]

        def scatter(i):
            peer = lax.rem(d + i, n_d)
            return pltpu.make_async_remote_copy(
                src_ref=buf.at[pl.ds(pl.multiple_of(peer * size, size), size)],
                dst_ref=rs.at[i - 1],
                send_sem=send1.at[base, i - 1], recv_sem=recv1.at[base, i - 1],
                device_id={"dp": peer}, device_id_type=MESH,
            )

        def across(axis, i):
            at = axis * 3 + i - 1
            return pltpu.make_async_remote_copy(
                src_ref=part.at[axis], dst_ref=lines.at[axis, place_y if axis else place_x],
                send_sem=send2.at[base, at], recv_sem=recv2.at[base, at],
                device_id={"space": along(axis, i)}, device_id_type=MESH,
            )

        def line_start(axis, total):
            part[axis] = total
            lines[axis, place_y if axis else place_x] = total
            for i in range(1, 4):
                across(axis, i).start()

        def line_sum(axis):
            for i in range(1, 4):
                across(axis, i).wait()
            return (lines[axis, 0] + lines[axis, 1]) + (lines[axis, 2] + lines[axis, 3])

        mine = pl.ds(pl.multiple_of(d * size, size), size)

        def around(i):
            return pltpu.make_async_remote_copy(
                src_ref=out.at[mine], dst_ref=out.at[mine],
                send_sem=send3.at[base, i - 1], recv_sem=recv3.at[base, i - 1],
                device_id={"dp": lax.rem(d + i, n_d)}, device_id_type=MESH,
            )

        def step1():
            for i in range(1, n_d):
                scatter(i).start()

        def step2():
            for i in range(1, n_d):
                scatter(i).wait()
            total = buf[mine, :]
            for i in range(1, n_d):
                total = total + rs[i - 1]
            line_start(0, total)

        def step3():
            line_start(1, line_sum(0))

        def step4():
            out[mine, :] = line_sum(1) * (1.0 / (n_s * n_d))
            for i in range(1, n_d):
                around(i).start()

        def step5():
            for i in range(1, n_d):
                around(i).wait()
            return [out[pl.ds(b, 8, stride=size), :] for b in range(blocks)]

        return step1, step2, step3, step4, step5

    def forward(first, last):
        @pl.loop(first, last)
        def _(k):
            rim_wait(1, k)

            stencil(1, k, halo_p, proj, sm)

    steps = reduce_all(left, 12, 16, p_buf, p_rs, p_part, p_all, p_out, 0)
    steps[0]()
    rims_start(0, 3, 5)
    project(0, 1)
    backward(0, 2)
    steps[1]()
    rims_start(0, 5, 6)
    project(1, 2)
    backward(2, 3)
    steps[2]()
    rims_start(0, 6, 8)
    backward(3, 6)
    steps[3]()
    rims_start(1, 0, 2)
    backward(6, 8)
    columns = steps[4]()

    at_row = lax.broadcasted_iota(jnp.int32, (8, 128), 0)
    for i in range(8):
        total = None
        lead = [x[i : i + 1, :] for x in columns]
        for x, y in zip(columns, lead):
            total = x * y if total is None else total + x * y
        dots = jnp.sum(total, axis=1, keepdims=True)
        scale = 1.0 / jnp.sqrt(dots[i : i + 1, :] + 1e-06)
        take = jnp.where(at_row[:, :1] > i, dots * scale, 0.0)
        lead = [y * scale for y in lead]
        columns = [jnp.where(at_row == i, y, x - take * y) for x, y in zip(columns, lead)]
    basis = jnp.concatenate(columns, axis=1)
    basis_ref[...] = basis

    rims_start(1, 2, 4)
    b16 = stacked(basis)
    z = fold(nt(b16, feats[...]))
    right = fold(jnp.dot(stacked(z), gp[...].reshape(2048, 512), preferred_element_type=F32))
    right = right + fold(jnp.dot(b16, error_high[...], preferred_element_type=F32))
    right = right + fold(jnp.dot(b16, error_low[...], preferred_element_type=F32))
    steps = reduce_all(right, 4, 8, r_buf, r_rs, r_part, r_all, r_out, 1)
    steps[0]()

    def gradient(first, last):
        @pl.loop(first, last)
        def _(i):
            at = pl.ds(pl.multiple_of(i * 768, 768), 768)
            tn = (((0,), (0,)), ((), ()))
            block = lax.dot_general(feats[:, at], gp[...].reshape(2048, 512), tn, preferred_element_type=F32)
            matrix[at, :] = block + error[at, :]

    gradient(0, 2)
    steps[1]()
    rims_start(1, 4, 5)
    forward(0, 3)
    steps[2]()
    rims_start(1, 5, 8)
    forward(3, 6)
    steps[3]()
    forward(6, 8)
    qt_ref[...] = jnp.concatenate(steps[4](), axis=1)


def final_kernel(
    gp, sm, matrix, lateral, basis, qt,
    smoothed, grad_feats, q_next, update, error_next,
    feats_v, error_v, full_v, small_sem, feats_sem, error_sem,
):
    cp_sm = pltpu.make_async_copy(sm, smoothed, small_sem.at[0])
    cp_sm.start()
    b, q = basis[...], qt[...]
    b_high, q_high = b.astype(BF).astype(F32), q.astype(BF).astype(F32)
    b24 = jnp.concatenate([b_high, b - b_high, b_high], axis=0).astype(BF)
    q24 = jnp.concatenate([q_high, q_high, q - q_high], axis=0).astype(BF)
    q_next[...] = q
    s = lax.axis_index("space")
    tn = (((0,), (0,)), ((), ()))

    def feats_copy(i):
        rows = pl.ds(i * 512, 512)
        return pltpu.make_async_copy(feats_v.at[rows], grad_feats.at[rows], feats_sem.at[i])

    def error_copy(i):
        rows = pl.ds(i * 384, 384)
        return pltpu.make_async_copy(error_v.at[rows], error_next.at[rows], error_sem.at[i])

    for i in range(4):
        cells = gp[i // 2, (i % 2) * 4 : (i % 2) * 4 + 4].reshape(512, 512)
        feats_v[i * 512 : (i + 1) * 512, :] = nt(cells, lateral[...]).astype(BF)
        feats_copy(i).start()
        full = lax.dot_general(b24[:, i * 384 : (i + 1) * 384], q24, tn, preferred_element_type=F32)
        rows = slice(i * 384, (i + 1) * 384)
        error_v[rows, :] = matrix[rows, :] - full
        error_copy(i).start()

        @pl.when(s // 4 == i)
        def _():
            full_v[...] = full

    update[...] = full_v[pl.ds(pl.multiple_of(lax.rem(s, 4) * 96, 8), 96), :]
    cp_sm.wait()
    for i in range(4):
        feats_copy(i).wait()
        error_copy(i).wait()


def body(feats, lateral, kernel, grad_out, error, q_prev):
    dma = pltpu.SemaphoreType.DMA
    hbm = pl.BlockSpec(memory_space=pltpu.HBM)
    vmem = pl.BlockSpec(memory_space=pltpu.VMEM)
    gp, sm, matrix, weight, basis, qt = pl.pallas_call(
        main_kernel,
        out_shape=(
            pltpu.VMEM((2, 8, 128, 512), BF),
            pltpu.VMEM((2, 8, 128, 512), BF),
            pltpu.VMEM((1536, 512), F32),
            pltpu.VMEM((1536, 512), BF),
            pltpu.VMEM((8, 1536), F32),
            pltpu.VMEM((8, 512), F32),
        ),
        in_specs=[hbm] * 4 + [vmem] * 2,
        out_specs=(vmem,) * 6,
        scratch_shapes=[
            pltpu.VMEM((1536, 512), BF),
            pltpu.VMEM((1536, 512), BF),
            pltpu.VMEM((2048, 1536), BF),
            pltpu.VMEM((2, 8, 128, 512), BF),
            pltpu.VMEM((1536, 512), F32),
            pltpu.VMEM((2, 8, 128, 512), BF),
            pltpu.VMEM((2, 2, 3, 128, 512), BF),
            pltpu.VMEM((2, 2, 3, 128, 512), BF),
            pltpu.VMEM((LEAVES, EXT, 128), F32),
            pltpu.VMEM((LEAVES, 128, 128), F32),
            pltpu.VMEM((2, LEAVES, TAPS, 8, 512), F32),
            pltpu.VMEM((2, 392, 512), F32),
            pltpu.VMEM((392, 2048), F32),
            pltpu.VMEM((2, 14, 8, 128), F32),
            pltpu.VMEM((2, 2, 3, 8, 128), F32),
            pltpu.VMEM((128, 128), F32),
            pltpu.VMEM((7, 16, 128), F32),
            pltpu.VMEM((2, 16, 128), F32),
            pltpu.VMEM((2, 4, 16, 128), F32),
            pltpu.VMEM((128, 128), F32),
            pltpu.VMEM((64, 128), F32),
            pltpu.VMEM((7, 8, 128), F32),
            pltpu.VMEM((2, 8, 128), F32),
            pltpu.VMEM((2, 4, 8, 128), F32),
            pltpu.VMEM((64, 128), F32),
            dma((3,)),
            dma((8,)),
            dma((32,)),
            dma((32,)),
            dma((2,)),
            dma((2,)),
            dma((2, 7)),
            dma((2, 7)),
            dma((2, 6)),
            dma((2, 6)),
            dma((2, 7)),
            dma((2, 7)),
        ],
        compiler_params=pltpu.CompilerParams(
            collective_id=0, has_side_effects=True, vmem_limit_bytes=48 * 2**20
        ),
        name="exchange",
    )(feats.reshape(2048, 1536), lateral, grad_out, error, kernel, q_prev.T)

    smoothed, grad_feats, q_next, update, error_next = pl.pallas_call(
        final_kernel,
        out_shape=(
            jax.ShapeDtypeStruct((2, 8, 128, 512), BF),
            jax.ShapeDtypeStruct((2048, 1536), BF),
            jax.ShapeDtypeStruct((8, 512), F32),
            jax.ShapeDtypeStruct((96, 512), F32),
            jax.ShapeDtypeStruct((1536, 512), F32),
        ),
        in_specs=[vmem] * 6,
        out_specs=(hbm, hbm, vmem, vmem, hbm),
        scratch_shapes=[
            pltpu.VMEM((2048, 1536), BF),
            pltpu.VMEM((1536, 512), F32),
            pltpu.VMEM((384, 512), F32),
            dma((1,)),
            dma((4,)),
            dma((4,)),
        ],
        compiler_params=pltpu.CompilerParams(vmem_limit_bytes=24 * 2**20),
        name="finish",
    )(gp, sm, matrix, weight, basis, qt)
    return smoothed, grad_feats.reshape(2, 8, 128, 1536), q_next.T, update, error_next


def solution(mesh):
    placed = (
        P("dp", "space", None, None),
        P(),
        P(),
        P("dp", "space", None, None),
        P(("dp", "space"), None),
        P(),
    )
    return jax.shard_map(
        body,
        mesh=mesh,
        in_specs=placed,
        out_specs=(
            P("dp", "space", None, None),
            P("dp", "space", None, None),
            P(),
            P("space", None),
            P(("dp", "space"), None),
        ),
        check_vma=False,
    )
```
